32 devices in a mesh: row: 4 (over y, core), col: 8 (over z, x).
Axes of the slice: x: 2, y: 2, z: 4, core: 2. Of those that a mesh axis runs over, the one named last changes fastest.
Arguments:
- shot_boxes: int32 [4, 4, 8192], P(None, 'row', 'col'), may hold values from 0 to 512, as said below
- block_counts: int32 [4, 8], P('row'), may hold values from 1 to 8, 32 in all within a row
- tail_shots: int32 [4, 8], P('row'), may hold values from 1 to 128
- doses: float32 [4, 8192], P('row', 'col'), may hold values from 0.5 to 1.5
- pixel_gain: float32 [2048, 4096], P('row', 'col'), may hold values from 0.6 to 1.6
Outputs:
- corrected: float32 [4, 8192], P('row', 'col')
- exposure: float32 [4, 8192], P('row', 'col')
The draws below stay inside these ranges and needn't reach their ends.
Inputs may be any that keep to these rules, and one draw needn't show every extreme that they name: `shot_boxes`: every shot has 8 <= x1 - x0 <= 64 and 8 <= y1 - y0 <= 64, inside its tile of 512 pixels. `block_counts`: in every tile row the block counts sum to exactly 32, and some tile of the row has 8.
All inputs are finite; a program needn't handle non-finite values.
Results may differ from the reference program's by a relative error of at most 0.0003.
Values sent between devices are 32-bit elements; how exact they have to be, the bound alone decides.
A program may use at most 64 MiB of HBM per device.

```python
import math
import jax
import jax.numpy as jnp
import numpy as np
from jax import lax

TILE = 512
CG = 128
BLK = 128
MAXB = 8
RCAP = 4
ITERS = 3
CELL = 4
BETA = 16
REACH = 32
WMAX = 64
SLOTS = 1024
NTR = 4
NTC = 8
N_COL = 8


def draw_shot_boxes(key, part):
    keys = jax.random.split(jax.random.fold_in(key, 17), 4)
    layout = (NTR, NTC * SLOTS)
    left_side = jax.random.randint(keys[0], layout, 0, TILE - WMAX + 1)
    top_side = jax.random.randint(keys[1], layout, 0, TILE - WMAX + 1)
    wide_side = jax.random.randint(keys[2], layout, 8, WMAX + 1)
    tall_side = jax.random.randint(keys[3], layout, 8, WMAX + 1)
    return jnp.stack([left_side, top_side, left_side + wide_side, top_side + tall_side]).astype(jnp.int32)


def plant(result, own_key, low, largest):
    extent = result.shape
    spot = [jax.random.randint(jax.random.fold_in(own_key, axis), (), 0, extent[axis]) for axis in range(len(extent))]
    result = result.at[tuple(spot)].set(low)
    longest = extent.index(max(extent))
    spot[longest] = (spot[longest] + 1) % extent[longest]
    return result.at[tuple(spot)].set(largest)


def steps_of(rng, dims, cuts, least, high):
    def one(dim, parts):
        steps = jax.random.uniform(jax.random.fold_in(jax.random.fold_in(rng, 6), dim), (parts,), jnp.float32, least / len(cuts), high / len(cuts))
        return jnp.repeat(jnp.exp(steps), dims[dim] // parts).reshape((-1,) + (1,) * (len(dims) - dim - 1))

    level = one(*cuts[0])
    for cut in cuts[1:]:
        level = level * one(*cut)
    return level


def profile(count, total, most, slope):
    portions = [(1 << 20) // math.isqrt(grade ** slope) + 1 for grade in range(2, count + 1)]
    rest, counts = total - most - (count - 1), [1] * (count - 1)
    while rest > 0:
        candidates = [i for i in range(count - 1) if counts[i] < most]
        whole, remaining = sum([portions[i] for i in candidates]), rest
        for i in candidates:
            addition = min(most - counts[i], max(1, remaining * portions[i] // whole), rest)
            counts[i] = counts[i] + addition
            rest = rest - addition
    return np.array([most] + counts)


def uneven_parts(key, number_of, total, limit, lean):
    if number_of == 2:
        one = jax.random.randint(key, (), max(1, total - limit), min(limit, total - 1) + 1)
        return jnp.stack([one, total - one])
    tallies = jnp.asarray(profile(number_of, total, limit, lean), jnp.int32)
    couples = (number_of - 1) // 2
    source_of, receiver = tallies[1:1 + 2 * couples:2], tallies[2:2 + 2 * couples:2]
    room = jnp.minimum(source_of - 1, limit - receiver)
    shifted = jax.random.randint(jax.random.fold_in(key, 1), (couples,), 0, 1 << 20) % (room + 1)
    tallies = tallies.at[1:1 + 2 * couples:2].set(source_of - shifted).at[2:2 + 2 * couples:2].set(receiver + shifted)
    return tallies[jax.random.permutation(jax.random.fold_in(key, 2), number_of)]


def setup_inputs(seed: int = 0) -> dict:
    streams_of = jax.random.split(jax.random.key(seed), 6)
    return {
        "shot_boxes": draw_shot_boxes(jax.random.fold_in(streams_of[5], 71), 0),
        "block_counts": jax.vmap(lambda own: uneven_parts(own, NTC, RCAP * N_COL, MAXB, 2))(jax.random.split(streams_of[1], NTR)).reshape((NTR, NTC)).astype(jnp.int32),
        "tail_shots": plant(jax.random.randint(streams_of[2], (NTR, NTC), 1, BLK + 1), jax.random.fold_in(streams_of[2], 1), 1, BLK).astype(jnp.int32),
        "doses": jnp.clip(0.5 + 1.0 * jax.random.uniform(streams_of[3], (NTR, NTC * SLOTS), jnp.float32) ** steps_of(streams_of[3], (NTR, NTC * SLOTS), ((0, 4), (1, 8)), -0.2, 0.2), 0.5, 1.5),
        "pixel_gain": jnp.clip(jnp.exp(math.log(1.6) - 0.98082923 * jax.random.uniform(streams_of[4], (NTR * TILE, NTC * TILE), jnp.float32) ** steps_of(streams_of[4], (NTR * TILE, NTC * TILE), ((0, 4), (1, 8)), -0.2, 0.2)), 0.6, 1.6),
    }


FORWARD_RANGE = 4.0
BACK_RATIO = 0.75
TARGET_LEVEL = 1.0
EXACT_MODE = lax.Precision.HIGHEST

def edge_term(doubled, low_edge, high_edge):
    middle = doubled.astype(jnp.float32)[None, :] * 0.5
    low_side = low_edge.astype(jnp.float32)[:, None]
    high_side = high_edge.astype(jnp.float32)[:, None]
    return 0.5 * (jax.scipy.special.erf((middle - low_side) / FORWARD_RANGE) - jax.scipy.special.erf((middle - high_side) / FORWARD_RANGE))

def pair_kernel(sources, centres):
    return edge_term(centres[0], sources[0], sources[2]) * edge_term(centres[1], sources[1], sources[3])

def intersection(low_edge, high_edge):
    cell_edges = jnp.arange(CG, dtype=jnp.int32) * CELL
    covered = jnp.minimum(high_edge[:, None], cell_edges[None, :] + CELL) - jnp.maximum(low_edge[:, None], cell_edges[None, :])
    return jnp.maximum(covered, 0).astype(jnp.float32) / CELL

def spread(distance):
    scaled = distance.astype(jnp.float32) / BETA
    inside = jnp.abs(distance) <= REACH
    return jnp.where(inside, jnp.exp(-scaled * scaled) / (math.sqrt(math.pi) * BETA), 0.0)

def tile_kernel(packed):
    return pair_kernel(packed[0], packed[1])

def reference(shot_boxes, block_counts, tail_shots, doses, pixel_gain):
    tile_count = NTR * NTC
    tiles = jnp.transpose(shot_boxes.reshape(4, NTR, NTC, SLOTS), (1, 2, 0, 3)).reshape(tile_count, 4, SLOTS)
    totals = ((block_counts - 1) * BLK + tail_shots).reshape(tile_count)
    is_live = jnp.arange(SLOTS, dtype=jnp.int32)[None, :] < totals[:, None]
    shot_dose = jnp.where(is_live, doses.reshape(tile_count, SLOTS), 0.0)
    centres = jnp.stack([tiles[:, 0] + tiles[:, 2], tiles[:, 1] + tiles[:, 3]], axis=1)
    kernels = lax.map(tile_kernel, (tiles, centres))
    across = jax.vmap(intersection)(tiles[:, 0], tiles[:, 2])
    downward = jax.vmap(intersection)(tiles[:, 1], tiles[:, 3])
    cell_ids = centres[:, 1] // (2 * CELL) * CG + centres[:, 0] // (2 * CELL)
    pixel_ids = (centres[:, 1] // 2 * TILE + centres[:, 0] // 2).astype(jnp.int32)
    gain_tiles = jnp.transpose(pixel_gain.reshape(NTR, TILE, NTC, TILE), (0, 2, 1, 3)).reshape(tile_count, TILE * TILE)
    sensitive = jnp.take_along_axis(gain_tiles, pixel_ids, axis=1)
    row_cells = jnp.arange(NTR * CG, dtype=jnp.int32)
    col_cells = jnp.arange(NTC * CG, dtype=jnp.int32)
    row_blur = spread(row_cells[:, None] - row_cells[None, :])
    col_blur = spread(col_cells[:, None] - col_cells[None, :])
    exposure = jnp.zeros_like(shot_dose)
    for sweep in range(ITERS):
        forward = jnp.einsum('nj,nji->ni', shot_dose, kernels, precision=EXACT_MODE)
        coarse = jnp.einsum('nsy,nsx->nyx', downward, shot_dose[:, :, None] * across, precision=EXACT_MODE)
        window = jnp.transpose(coarse.reshape(NTR, NTC, CG, CG), (0, 2, 1, 3)).reshape(NTR * CG, NTC * CG)
        blurred = jnp.dot(row_blur, window, precision=EXACT_MODE)
        background = jnp.dot(blurred, col_blur, precision=EXACT_MODE)
        tile_maps = jnp.transpose(background.reshape(NTR, CG, NTC, CG), (0, 2, 1, 3)).reshape(tile_count, CG * CG)
        sampled = jnp.take_along_axis(tile_maps, cell_ids, axis=1)
        exposure = sensitive * (forward + BACK_RATIO * sampled) / (1.0 + BACK_RATIO)
        shot_dose = jnp.where(is_live, shot_dose * TARGET_LEVEL / jnp.where(is_live, exposure, 1.0), 0.0)
    corrected = shot_dose.reshape(NTR, NTC * SLOTS)
    final_exposure = jnp.where(is_live, exposure, 0.0).reshape(NTR, NTC * SLOTS)
    return (corrected, final_exposure)
```

```python
import functools
import math

import jax
import jax.numpy as jnp
from jax import lax
from jax.experimental import pallas as pl
from jax.experimental.pallas import tpu as pltpu
from jax.sharding import PartitionSpec as P

BLK = 128
ITERS = 3
CELL = 4
BETA = 16
REACH = 32
LANES = 128

FORWARD_RANGE = 4.0
BACK_RATIO = 0.75
TARGET_LEVEL = 1.0
MESH = pl.DeviceIdType.MESH
NEAR = [(-1, 0), (1, 0), (0, -1), (0, 1), (-1, -1), (-1, 1), (1, -1), (1, 1)]


def halves(value):
    high = value.astype(jnp.bfloat16)
    low = (value - high.astype(jnp.float32)).astype(jnp.bfloat16)
    return high, low


def mxu(a, b):
    return jnp.dot(a, b, preferred_element_type=jnp.float32)


def spread(distance):
    scaled = distance.astype(jnp.float32) / BETA
    inside = jnp.abs(distance) <= REACH
    return jnp.where(inside, jnp.exp(-scaled * scaled) / (math.sqrt(math.pi) * BETA), 0.0)


def covered(low, high, cell):
    edge = cell.astype(jnp.float32) * CELL
    part = jnp.minimum(high, edge + CELL) - jnp.maximum(low, edge)
    return jnp.maximum(part, 0.0) * (1.0 / CELL)


def kernel(
    rows, cols,
    boxes, counts, tails, doses, gain_hbm, dose_out, exposure_out,
    gain, gain2, pairs, column, dose_column, down_t, side_t, across, downward,
    wx2, wy2, wy_own, wy_halo, wx_halo, sens,
    coarse, coarse_t, corner_out, halo_y, halo_x, corner_in,
    gain_sem, send_sem, recv_sem,
):
    slots = doses.shape[1]
    tile = gain.shape[0]
    cg = tile // CELL
    r, c = lax.axis_index("row"), lax.axis_index("col")
    halo_y[...] = jnp.zeros_like(halo_y)
    halo_x[...] = jnp.zeros_like(halo_x)
    corner_in[...] = jnp.zeros_like(corner_in)

    def present(dr, dc):
        tests = []
        if dr:
            tests.append(r > 0 if dr < 0 else r < rows - 1)
        if dc:
            tests.append(c > 0 if dc < 0 else c < cols - 1)
        return functools.reduce(jnp.logical_and, tests)

    barrier = pltpu.get_barrier_semaphore()
    for dr, dc in NEAR:
        @pl.when(present(dr, dc))
        def _():
            pl.semaphore_signal(barrier, inc=1, device_id=(r + dr, c + dc), device_id_type=MESH)

    fetch = pltpu.make_async_copy(gain_hbm, gain, gain_sem)
    fetch.start()

    x0, y0, x1, y1 = (boxes[k].astype(jnp.float32) for k in range(4))
    peers = lax.broadcasted_iota(jnp.int32, counts.shape, 1)
    totals = (counts[...] - 1) * BLK + tails[...]
    total = jnp.sum(jnp.where(peers == c, totals, 0), axis=1, keepdims=True)
    live = lax.broadcasted_iota(jnp.int32, (1, slots), 1) < total
    dose = jnp.where(live, doses[...], 0.0)

    stack = jnp.concatenate([x0, x1, y0, y1, dose, dose, dose, dose], axis=0)
    column[...] = jnp.transpose(stack)
    cell_row = lax.broadcasted_iota(jnp.int32, (slots, cg), 1)
    downward[...] = covered(column[:, 2:3], column[:, 3:4], cell_row).astype(jnp.bfloat16)
    side = lax.broadcasted_iota(jnp.int32, (2 * REACH, slots), 0)
    side = jnp.where(side < REACH, side, side + (cg - 2 * REACH))
    side_t[...] = covered(x0, x1, side)
    across[...] = covered(column[:, 0:1], column[:, 1:2], cell_row).astype(jnp.bfloat16)
    down_t[...] = covered(y0, y1, lax.broadcasted_iota(jnp.int32, (cg, slots), 0))
    lane = lax.broadcasted_iota(jnp.int32, (8, LANES), 1)

    def copies(k):
        made = []
        for n, (dr, dc) in enumerate(NEAR):
            ys, xs = (0 if dr < 0 else 1), (0 if dc < 0 else 1)
            if dc == 0:
                src = coarse.at[k, pl.ds(ys * (cg - REACH), REACH), :]
                dst = halo_y.at[k, pl.ds((1 - ys) * REACH, REACH), :]
            elif dr == 0:
                src = coarse_t.at[k, pl.ds(xs * REACH, REACH), :]
                dst = halo_x.at[k, pl.ds((1 - xs) * REACH, REACH), :]
            else:
                src = corner_out.at[k, 2 * xs + ys]
                dst = corner_in.at[k, 2 * (1 - xs) + (1 - ys)]
            made.append(pltpu.make_async_remote_copy(
                src_ref=src, dst_ref=dst,
                send_sem=send_sem.at[k, n], recv_sem=recv_sem.at[k, n],
                device_id=(r + dr, c + dc), device_id_type=MESH,
            ))
        return made

    def send(k, dose, first):
        high, low = halves(side_t[...] * dose)
        both = mxu(jnp.concatenate([high, low], axis=0), downward[...])
        edges = both[:2 * REACH] + both[2 * REACH:]
        coarse_t[k] = edges
        for xs in range(2):
            for ys in range(2):
                packed = jnp.zeros((8, LANES), jnp.float32)
                for q in range(REACH // 8):
                    part = edges[xs * REACH + 8 * q:xs * REACH + 8 * q + 8]
                    shift = (REACH * q - ys * (cg - REACH)) % LANES
                    if shift:
                        part = pltpu.roll(part, shift, 1)
                    packed = jnp.where(lane // REACH == q, part, packed)
                corner_out[k, 2 * xs + ys] = packed
        made = copies(k)
        if first:
            up = (r > 0).astype(jnp.int32) + (r < rows - 1).astype(jnp.int32) + 1
            across_count = (c > 0).astype(jnp.int32) + (c < cols - 1).astype(jnp.int32) + 1
            pl.semaphore_wait(barrier, up * across_count - 1)
        for n in range(2, 8):
            @pl.when(present(*NEAR[n]))
            def _():
                made[n].start()
        high, low = halves(down_t[...] * dose)
        both = mxu(jnp.concatenate([high, low], axis=0), across[...])
        coarse[k] = both[:cg] + both[cg:]
        for n in range(2):
            @pl.when(present(*NEAR[n]))
            def _():
                made[n].start()
        return made

    def weighted(value, weights2, weights):
        high, low = halves(value)
        lhs = jnp.concatenate(
            [jnp.concatenate([high, high], axis=1), jnp.concatenate([low, low], axis=1)], axis=0
        )
        both = mxu(lhs, weights2[...])
        count = value.shape[0]
        return jnp.sum((both[:count] + both[count:]) * weights[...], axis=0, keepdims=True)

    made = send(0, dose, True)

    two_x, two_y = boxes[0] + boxes[2], boxes[1] + boxes[3]
    cell_x, cell_y = two_x >> 3, two_y >> 3
    own = lax.broadcasted_iota(jnp.int32, (cg, slots), 0)
    around = lax.broadcasted_iota(jnp.int32, (2 * REACH, slots), 0)
    around = jnp.where(around < REACH, around - REACH, around + (cg - REACH))
    high, low = halves(spread(own - cell_x))
    wx2[0:cg, :] = high
    wx2[cg:2 * cg, :] = low
    weight = spread(own - cell_y)
    wy_own[...] = weight
    high, low = halves(weight)
    wy2[0:cg, :] = high
    wy2[2 * cg:3 * cg, :] = low
    weight = spread(around - cell_y)
    wy_halo[...] = weight
    high, low = halves(weight)
    blank = jnp.zeros((cg - 2 * REACH, slots), jnp.bfloat16)
    wy2[cg:2 * cg, :] = jnp.concatenate([high, blank], axis=0)
    wy2[3 * cg:4 * cg, :] = jnp.concatenate([low, blank], axis=0)
    wx_halo[...] = spread(around - cell_x)

    table = 0.5 * lax.erf((lane - LANES // 2).astype(jnp.float32) * (0.5 / FORWARD_RANGE))

    def look(index):
        index = jnp.clip(index, 0, LANES - 1)
        return jnp.take_along_axis(table, index, axis=1, mode="promise_in_bounds")

    blocks = slots // LANES
    half = LANES // 2

    def build(g, totals):
        start = pl.multiple_of(g * 8, 8)
        group = column[pl.ds(start, 8), :]
        wide = [
            jnp.broadcast_to(group[:, m:m + 1], (8, LANES)) for m in range(5)
        ]
        bx0, bx1, by0, by1 = (w.astype(jnp.int32) * 2 - half for w in wide[:4])
        fresh = []
        for b in range(blocks):
            at = slice(b * LANES, (b + 1) * LANES)
            px = jnp.broadcast_to(two_x[:, at], (8, LANES))
            py = jnp.broadcast_to(two_y[:, at], (8, LANES))
            gx = look(px - bx0) - look(px - bx1)
            gy = look(py - by0) - look(py - by1)
            value = gx * gy
            pairs[pl.ds(start, 8), at] = value
            fresh.append(totals[b] + value * wide[4])
        return tuple(fresh)

    zero = tuple(jnp.zeros((8, LANES), jnp.float32) for _ in range(blocks))
    sums = lax.fori_loop(0, slots // 8, build, zero)
    forward = jnp.concatenate([jnp.sum(s, axis=0, keepdims=True) for s in sums], axis=1)

    fetch.wait()
    high, low = halves(gain[...])
    gain2[:, 0:tile] = high
    gain2[:, tile:2 * tile] = low
    step = 256

    def sample(i, _):
        at = pl.ds(pl.multiple_of(i * step, step), step)
        mid_x = (boxes[0, :, at] + boxes[2, :, at]) >> 1
        mid_y = (boxes[1, :, at] + boxes[3, :, at]) >> 1
        pixel = lax.broadcasted_iota(jnp.int32, (tile, step), 0)
        hot = jnp.where(pixel == mid_x, 1.0, 0.0).astype(jnp.bfloat16)
        taken = mxu(gain2[...], jnp.concatenate([hot, hot], axis=0))
        sens[:, at] = jnp.sum(jnp.where(pixel == mid_y, taken, 0.0), axis=0, keepdims=True)
        return 0

    lax.fori_loop(0, slots // step, sample, 0)

    for k in range(ITERS):
        if k:
            made = send(k, dose, False)
            dose_column[...] = jnp.transpose(jnp.broadcast_to(dose, (8, slots)))

            def add(g, totals):
                start = pl.multiple_of(g * 8, 8)
                wide = jnp.broadcast_to(dose_column[pl.ds(start, 8), 0:1], (8, LANES))
                return tuple(
                    totals[b] + pairs[pl.ds(start, 8), b * LANES:(b + 1) * LANES] * wide
                    for b in range(blocks)
                )

            sums = lax.fori_loop(0, slots // 8, add, zero, unroll=4)
            forward = jnp.concatenate([jnp.sum(s, axis=0, keepdims=True) for s in sums], axis=1)
        background = weighted(coarse[k], wx2, wy_own)
        for n, (dr, dc) in enumerate(NEAR):
            @pl.when(present(-dr, -dc))
            def _():
                made[n].wait_recv()
        background += weighted(halo_y[k], wx2, wy_halo)
        strips = []
        for xs in range(2):
            for q in range(REACH // 8):
                top, low_part = corner_in[k, 2 * xs], corner_in[k, 2 * xs + 1]
                shift = (-REACH * q) % LANES
                if shift:
                    top = pltpu.roll(top, shift, 1)
                shift = (REACH - REACH * q) % LANES
                if shift:
                    low_part = pltpu.roll(low_part, shift, 1)
                strips.append(jnp.where(
                    lane < REACH, top, jnp.where(lane < 2 * REACH, low_part, 0.0)
                ))
        sides = jnp.concatenate([halo_x[k], jnp.concatenate(strips, axis=0)], axis=1)
        background += weighted(sides, wy2, wx_halo)
        exposure = sens[...] * (forward + BACK_RATIO * background) * (1.0 / (1.0 + BACK_RATIO))
        dose = jnp.where(live, dose * TARGET_LEVEL / jnp.where(live, exposure, 1.0), 0.0)
    dose_out[...] = dose
    exposure_out[...] = jnp.where(live, exposure, 0.0)
    for k in range(ITERS):
        made = copies(k)
        for n in range(8):
            @pl.when(present(*NEAR[n]))
            def _():
                made[n].wait_send()


def body(rows, cols, shot_boxes, block_counts, tail_shots, doses, pixel_gain):
    slots = doses.shape[1]
    tile = pixel_gain.shape[0]
    cg = tile // CELL
    f32, bf16 = jnp.float32, jnp.bfloat16
    vmem = pl.BlockSpec(memory_space=pltpu.VMEM)
    return pl.pallas_call(
        functools.partial(kernel, rows, cols),
        out_shape=(jax.ShapeDtypeStruct((1, slots), f32),) * 2,
        in_specs=[vmem] * 4 + [pl.BlockSpec(memory_space=pl.ANY)],
        out_specs=(vmem, vmem),
        scratch_shapes=[
            pltpu.VMEM((tile, tile), f32),
            pltpu.VMEM((tile, 2 * tile), bf16),
            pltpu.VMEM((slots, slots), f32),
            pltpu.VMEM((slots, 8), f32),
            pltpu.VMEM((slots, 8), f32),
            pltpu.VMEM((cg, slots), f32),
            pltpu.VMEM((2 * REACH, slots), f32),
            pltpu.VMEM((slots, cg), bf16),
            pltpu.VMEM((slots, cg), bf16),
            pltpu.VMEM((2 * cg, slots), bf16),
            pltpu.VMEM((4 * cg, slots), bf16),
            pltpu.VMEM((cg, slots), f32),
            pltpu.VMEM((2 * REACH, slots), f32),
            pltpu.VMEM((2 * REACH, slots), f32),
            pltpu.VMEM((1, slots), f32),
            pltpu.VMEM((ITERS, cg, cg), f32),
            pltpu.VMEM((ITERS, 2 * REACH, cg), f32),
            pltpu.VMEM((ITERS, 4, 8, LANES), f32),
            pltpu.VMEM((ITERS, 2 * REACH, cg), f32),
            pltpu.VMEM((ITERS, 2 * REACH, cg), f32),
            pltpu.VMEM((ITERS, 4, 8, LANES), f32),
            pltpu.SemaphoreType.DMA,
            pltpu.SemaphoreType.DMA((ITERS, 8)),
            pltpu.SemaphoreType.DMA((ITERS, 8)),
        ],
        compiler_params=pltpu.CompilerParams(
            collective_id=0, has_side_effects=True, vmem_limit_bytes=40 * 1024 * 1024
        ),
    )(shot_boxes, block_counts, tail_shots, doses, pixel_gain)


def solution(mesh):
    placed = (
        P(None, "row", "col"),
        P("row", None),
        P("row", None),
        P("row", "col"),
        P("row", "col"),
    )
    return jax.shard_map(
        functools.partial(body, mesh.shape["row"], mesh.shape["col"]),
        mesh=mesh,
        in_specs=placed,
        out_specs=(P("row", "col"), P("row", "col")),
        check_vma=False,
    )
```

```python
import functools
import math

import jax
import jax.numpy as jnp
from jax import lax
from jax.experimental import pallas as pl
from jax.experimental.pallas import tpu as pltpu
from jax.sharding import PartitionSpec as P

BLK = 128
ITERS = 3
CELL = 4
BETA = 16
REACH = 32
LANES = 128
EDGE_STEP = 16
UNROLL = 16

FORWARD_RANGE = 4.0
BACK_RATIO = 0.75
TARGET_LEVEL = 1.0
MESH = pl.DeviceIdType.MESH
NEAR = [(-1, 0), (1, 0), (0, -1), (0, 1), (-1, -1), (-1, 1), (1, -1), (1, 1)]


def halves(value):
    high = value.astype(jnp.bfloat16)
    low = (value - high.astype(jnp.float32)).astype(jnp.bfloat16)
    return high, low


def mxu(a, b):
    return jnp.dot(a, b, preferred_element_type=jnp.float32)


def spread(distance):
    scaled = distance.astype(jnp.float32) / BETA
    inside = jnp.abs(distance) <= REACH
    return jnp.where(inside, jnp.exp(-scaled * scaled) / (math.sqrt(math.pi) * BETA), 0.0)


def covered(low, high, cell):
    edge = cell.astype(jnp.float32) * CELL
    part = jnp.minimum(high, edge + CELL) - jnp.maximum(low, edge)
    return jnp.maximum(part, 0.0) * (1.0 / CELL)


def kernel(
    rows, cols,
    box_scalar, boxes_hbm, counts_hbm, tails_hbm, doses_hbm, gain_hbm, dose_out, exposure_out,
    boxes, counts, tails, doses, near_x, near_y, edge_x, edge_y, dose_wide,
    gain, gain2, pairs, column, down_t, side_t, across, downward,
    wx2, wy2, wy_own, wy_halo, wx_halo, sens,
    coarse, coarse_t, corner_out, halo_y, halo_x, corner_in,
    in_sem, send_sem, recv_sem,
):
    slots = doses.shape[1]
    tile = gain.shape[0]
    cg = tile // CELL
    r, c = lax.axis_index("row"), lax.axis_index("col")
    halo_y[...] = jnp.zeros_like(halo_y)
    halo_x[...] = jnp.zeros_like(halo_x)
    corner_in[...] = jnp.zeros_like(corner_in)

    def present(dr, dc):
        tests = []
        if dr:
            tests.append(r > 0 if dr < 0 else r < rows - 1)
        if dc:
            tests.append(c > 0 if dc < 0 else c < cols - 1)
        return functools.reduce(jnp.logical_and, tests)

    barrier = pltpu.get_barrier_semaphore()
    for dr, dc in NEAR:
        @pl.when(present(dr, dc))
        def _():
            pl.semaphore_signal(barrier, inc=1, device_id=(r + dr, c + dc), device_id_type=MESH)

    fetches = [
        pltpu.make_async_copy(src, dst, in_sem.at[n])
        for n, (src, dst) in enumerate((
            (boxes_hbm, boxes), (counts_hbm, counts), (tails_hbm, tails), (doses_hbm, doses),
            (gain_hbm, gain),
        ))
    ]
    fetch = fetches[4]
    for one in fetches[:4]:
        one.start()
    fetch.start()
    for one in fetches[:4]:
        one.wait()

    x0, y0, x1, y1 = (boxes[k].astype(jnp.float32) for k in range(4))
    peers = lax.broadcasted_iota(jnp.int32, counts.shape, 1)
    totals = (counts[...] - 1) * BLK + tails[...]
    total = jnp.sum(jnp.where(peers == c, totals, 0), axis=1, keepdims=True)
    live = lax.broadcasted_iota(jnp.int32, (1, slots), 1) < total
    dose = jnp.where(live, doses[...], 0.0)

    stack = jnp.concatenate([x0, x1, y0, y1, dose, dose, dose, dose], axis=0)
    column[...] = jnp.transpose(stack)
    cell_row = lax.broadcasted_iota(jnp.int32, (slots, cg), 1)
    downward[...] = covered(column[:, 2:3], column[:, 3:4], cell_row).astype(jnp.bfloat16)
    side = lax.broadcasted_iota(jnp.int32, (2 * REACH, slots), 0)
    side = jnp.where(side < REACH, side, side + (cg - 2 * REACH))
    side_t[...] = covered(x0, x1, side)
    across[...] = covered(column[:, 0:1], column[:, 1:2], cell_row).astype(jnp.bfloat16)
    down_t[...] = covered(y0, y1, lax.broadcasted_iota(jnp.int32, (cg, slots), 0))
    lane = lax.broadcasted_iota(jnp.int32, (8, LANES), 1)

    def copies(k):
        made = []
        for n, (dr, dc) in enumerate(NEAR):
            ys, xs = (0 if dr < 0 else 1), (0 if dc < 0 else 1)
            if dc == 0:
                src = coarse.at[k, pl.ds(ys * (cg - REACH), REACH), :]
                dst = halo_y.at[k, pl.ds((1 - ys) * REACH, REACH), :]
            elif dr == 0:
                src = coarse_t.at[k, pl.ds(xs * REACH, REACH), :]
                dst = halo_x.at[k, pl.ds((1 - xs) * REACH, REACH), :]
            else:
                src = corner_out.at[k, 2 * xs + ys]
                dst = corner_in.at[k, 2 * (1 - xs) + (1 - ys)]
            made.append(pltpu.make_async_remote_copy(
                src_ref=src, dst_ref=dst,
                send_sem=send_sem.at[k, n], recv_sem=recv_sem.at[k, n],
                device_id=(r + dr, c + dc), device_id_type=MESH,
            ))
        return made

    def send(k, dose, first):
        high, low = halves(side_t[...] * dose)
        both = mxu(jnp.concatenate([high, low], axis=0), downward[...])
        edges = both[:2 * REACH] + both[2 * REACH:]
        coarse_t[k] = edges
        for xs in range(2):
            for ys in range(2):
                packed = jnp.zeros((8, LANES), jnp.float32)
                for q in range(REACH // 8):
                    part = edges[xs * REACH + 8 * q:xs * REACH + 8 * q + 8]
                    shift = (REACH * q - ys * (cg - REACH)) % LANES
                    if shift:
                        part = pltpu.roll(part, shift, 1)
                    packed = jnp.where(lane // REACH == q, part, packed)
                corner_out[k, 2 * xs + ys] = packed
        made = copies(k)
        if first:
            up = (r > 0).astype(jnp.int32) + (r < rows - 1).astype(jnp.int32) + 1
            across_count = (c > 0).astype(jnp.int32) + (c < cols - 1).astype(jnp.int32) + 1
            pl.semaphore_wait(barrier, up * across_count - 1)
        for n in range(2, 8):
            @pl.when(present(*NEAR[n]))
            def _():
                made[n].start()
        high, low = halves(down_t[...] * dose)
        both = mxu(jnp.concatenate([high, low], axis=0), across[...])
        coarse[k] = both[:cg] + both[cg:]
        for n in range(2):
            @pl.when(present(*NEAR[n]))
            def _():
                made[n].start()
        return made

    def weighted(value, weights2, weights):
        high, low = halves(value)
        lhs = jnp.concatenate(
            [jnp.concatenate([high, high], axis=1), jnp.concatenate([low, low], axis=1)], axis=0
        )
        both = mxu(lhs, weights2[...])
        count = value.shape[0]
        return jnp.sum((both[:count] + both[count:]) * weights[...], axis=0, keepdims=True)

    made = send(0, dose, True)

    two_x, two_y = boxes[0] + boxes[2], boxes[1] + boxes[3]
    cell_x, cell_y = two_x >> 3, two_y >> 3
    own = lax.broadcasted_iota(jnp.int32, (cg, slots), 0)
    around = lax.broadcasted_iota(jnp.int32, (2 * REACH, slots), 0)
    around = jnp.where(around < REACH, around - REACH, around + (cg - REACH))
    high, low = halves(spread(own - cell_x))
    wx2[0:cg, :] = high
    wx2[cg:2 * cg, :] = low
    weight = spread(own - cell_y)
    wy_own[...] = weight
    high, low = halves(weight)
    wy2[0:cg, :] = high
    wy2[2 * cg:3 * cg, :] = low
    weight = spread(around - cell_y)
    wy_halo[...] = weight
    high, low = halves(weight)
    blank = jnp.zeros((cg - 2 * REACH, slots), jnp.bfloat16)
    wy2[cg:2 * cg, :] = jnp.concatenate([high, blank], axis=0)
    wy2[3 * cg:4 * cg, :] = jnp.concatenate([low, blank], axis=0)
    wx_halo[...] = spread(around - cell_x)

    blocks = slots // LANES
    group = EDGE_STEP

    def folded(row):
        return jnp.concatenate([row[:, b * LANES:(b + 1) * LANES] for b in range(blocks)], axis=0)

    def flat(square):
        return jnp.concatenate([square[b:b + 1, :] for b in range(blocks)], axis=1)

    for two, near, edges in ((folded(two_x), near_x, edge_x), (folded(two_y), near_y, edge_y)):
        coarse_part = two // (2 * group)
        fine = two - coarse_part * (2 * group)
        for m in range(3):
            for q in range(group):
                gap = fine + ((m - 1) * 2 * group - 2 * q)
                near[m * group + q] = 0.5 * lax.erf(gap.astype(jnp.float32) * (0.5 / FORWARD_RANGE))

        def fill(p, _):
            same, above, below = coarse_part == p, coarse_part == p + 1, coarse_part == p - 1
            far = jnp.where(coarse_part > p, 0.5, -0.5)
            for q in range(group):
                value = jnp.where(above, near[2 * group + q], far)
                value = jnp.where(below, near[q], value)
                edges[p * group + q] = jnp.where(same, near[group + q], value)
            return 0

        lax.fori_loop(0, tile // group + 1, fill, 0)

    def widen(dose):
        for b in range(blocks):
            at = slice(b * LANES, (b + 1) * LANES)
            dose_wide[at, :] = jnp.transpose(jnp.broadcast_to(dose[:, at], (LANES, LANES)))

    zero = tuple(jnp.zeros((blocks, LANES), jnp.float32) for _ in range(4))

    def total_of(sums):
        return flat((sums[0] + sums[1]) + (sums[2] + sums[3]))

    def build(g, sums):
        sums = list(sums)
        kept = []
        for n in range(UNROLL):
            j = g * UNROLL + n
            low_x, low_y, high_x, high_y = (box_scalar[k, 0, j] for k in range(4))
            kept.append((edge_x[low_x] - edge_x[high_x]) * (edge_y[low_y] - edge_y[high_y]))
        for n in range(UNROLL):
            j = g * UNROLL + n
            pairs[j] = kept[n]
            sums[n % 4] += kept[n] * dose_wide[pl.ds(j, 1), :]
        return tuple(sums)

    widen(dose)
    forward = total_of(lax.fori_loop(0, slots // UNROLL, build, zero))

    fetch.wait()
    high, low = halves(gain[...])
    gain2[:, 0:tile] = high
    gain2[:, tile:2 * tile] = low
    step = 256

    def sample(i, _):
        at = pl.ds(pl.multiple_of(i * step, step), step)
        mid_x = (boxes[0, :, at] + boxes[2, :, at]) >> 1
        mid_y = (boxes[1, :, at] + boxes[3, :, at]) >> 1
        pixel = lax.broadcasted_iota(jnp.int32, (tile, step), 0)
        hot = jnp.where(pixel == mid_x, 1.0, 0.0).astype(jnp.bfloat16)
        taken = mxu(gain2[...], jnp.concatenate([hot, hot], axis=0))
        sens[:, at] = jnp.sum(jnp.where(pixel == mid_y, taken, 0.0), axis=0, keepdims=True)
        return 0

    lax.fori_loop(0, slots // step, sample, 0)

    for k in range(ITERS):
        if k:
            made = send(k, dose, False)
            widen(dose)

            def add(g, sums):
                sums = list(sums)
                for n in range(16):
                    j = g * 16 + n
                    sums[n % 4] += pairs[j] * dose_wide[pl.ds(j, 1), :]
                return tuple(sums)

            forward = total_of(lax.fori_loop(0, slots // 16, add, zero))
        background = weighted(coarse[k], wx2, wy_own)
        for n, (dr, dc) in enumerate(NEAR):
            @pl.when(present(-dr, -dc))
            def _():
                made[n].wait_recv()
        background += weighted(halo_y[k], wx2, wy_halo)
        strips = []
        for xs in range(2):
            for q in range(REACH // 8):
                top, low_part = corner_in[k, 2 * xs], corner_in[k, 2 * xs + 1]
                shift = (-REACH * q) % LANES
                if shift:
                    top = pltpu.roll(top, shift, 1)
                shift = (REACH - REACH * q) % LANES
                if shift:
                    low_part = pltpu.roll(low_part, shift, 1)
                strips.append(jnp.where(
                    lane < REACH, top, jnp.where(lane < 2 * REACH, low_part, 0.0)
                ))
        sides = jnp.concatenate([halo_x[k], jnp.concatenate(strips, axis=0)], axis=1)
        background += weighted(sides, wy2, wx_halo)
        exposure = sens[...] * (forward + BACK_RATIO * background) * (1.0 / (1.0 + BACK_RATIO))
        dose = jnp.where(live, dose * TARGET_LEVEL / jnp.where(live, exposure, 1.0), 0.0)
    dose_out[...] = dose
    exposure_out[...] = jnp.where(live, exposure, 0.0)
    for k in range(ITERS):
        made = copies(k)
        for n in range(8):
            @pl.when(present(*NEAR[n]))
            def _():
                made[n].wait_send()


def body(rows, cols, shot_boxes, block_counts, tail_shots, doses, pixel_gain):
    slots = doses.shape[1]
    tile = pixel_gain.shape[0]
    cg = tile // CELL
    f32, bf16 = jnp.float32, jnp.bfloat16
    vmem = pl.BlockSpec(memory_space=pltpu.VMEM)
    return pl.pallas_call(
        functools.partial(kernel, rows, cols),
        out_shape=(jax.ShapeDtypeStruct((1, slots), f32),) * 2,
        in_specs=[pl.BlockSpec(memory_space=pltpu.SMEM)]
        + [pl.BlockSpec(memory_space=pltpu.HBM)] * 5,
        out_specs=(vmem, vmem),
        scratch_shapes=[
            pltpu.VMEM(shot_boxes.shape, jnp.int32),
            pltpu.VMEM(block_counts.shape, jnp.int32),
            pltpu.VMEM(tail_shots.shape, jnp.int32),
            pltpu.VMEM(doses.shape, f32),
            pltpu.VMEM((3 * EDGE_STEP, slots // LANES, LANES), f32),
            pltpu.VMEM((3 * EDGE_STEP, slots // LANES, LANES), f32),
            pltpu.VMEM((tile + EDGE_STEP, slots // LANES, LANES), f32),
            pltpu.VMEM((tile + EDGE_STEP, slots // LANES, LANES), f32),
            pltpu.VMEM((slots, LANES), f32),
            pltpu.VMEM((tile, tile), f32),
            pltpu.VMEM((tile, 2 * tile), bf16),
            pltpu.VMEM((slots, slots // LANES, LANES), f32),
            pltpu.VMEM((slots, 8), f32),
            pltpu.VMEM((cg, slots), f32),
            pltpu.VMEM((2 * REACH, slots), f32),
            pltpu.VMEM((slots, cg), bf16),
            pltpu.VMEM((slots, cg), bf16),
            pltpu.VMEM((2 * cg, slots), bf16),
            pltpu.VMEM((4 * cg, slots), bf16),
            pltpu.VMEM((cg, slots), f32),
            pltpu.VMEM((2 * REACH, slots), f32),
            pltpu.VMEM((2 * REACH, slots), f32),
            pltpu.VMEM((1, slots), f32),
            pltpu.VMEM((ITERS, cg, cg), f32),
            pltpu.VMEM((ITERS, 2 * REACH, cg), f32),
            pltpu.VMEM((ITERS, 4, 8, LANES), f32),
            pltpu.VMEM((ITERS, 2 * REACH, cg), f32),
            pltpu.VMEM((ITERS, 2 * REACH, cg), f32),
            pltpu.VMEM((ITERS, 4, 8, LANES), f32),
            pltpu.SemaphoreType.DMA((5,)),
            pltpu.SemaphoreType.DMA((ITERS, 8)),
            pltpu.SemaphoreType.DMA((ITERS, 8)),
        ],
        compiler_params=pltpu.CompilerParams(
            collective_id=0, has_side_effects=True, vmem_limit_bytes=60 * 1024 * 1024
        ),
    )(shot_boxes, shot_boxes, block_counts, tail_shots, doses, pixel_gain)


def solution(mesh):
    placed = (
        P(None, "row", "col"),
        P("row", None),
        P("row", None),
        P("row", "col"),
        P("row", "col"),
    )
    return jax.shard_map(
        functools.partial(body, mesh.shape["row"], mesh.shape["col"]),
        mesh=mesh,
        in_specs=placed,
        out_specs=(P("row", "col"), P("row", "col")),
        check_vma=False,
    )
```

```python
import functools
import math

import jax
import jax.numpy as jnp
from jax import lax
from jax.experimental import pallas as pl
from jax.experimental.pallas import tpu as pltpu
from jax.sharding import PartitionSpec as P

BLK = 128
ITERS = 3
CELL = 4
BETA = 16
REACH = 32
LANES = 128
EDGE_STEP = 16
UNROLL = 16
STEP = 128

FORWARD_RANGE = 4.0
BACK_RATIO = 0.75
TARGET_LEVEL = 1.0
MESH = pl.DeviceIdType.MESH
NEAR = [(-1, 0), (1, 0), (0, -1), (0, 1), (-1, -1), (-1, 1), (1, -1), (1, 1)]


def halves(value):
    high = value.astype(jnp.bfloat16)
    low = (value - high.astype(jnp.float32)).astype(jnp.bfloat16)
    return high, low


def mxu(a, b):
    return jnp.dot(a, b, preferred_element_type=jnp.float32)


def spread(distance):
    scaled = distance.astype(jnp.float32) / BETA
    inside = jnp.abs(distance) <= REACH
    return jnp.where(inside, jnp.exp(-scaled * scaled) / (math.sqrt(math.pi) * BETA), 0.0)


def covered(low, high, cell):
    edge = cell.astype(jnp.float32) * CELL
    part = jnp.minimum(high, edge + CELL) - jnp.maximum(low, edge)
    return jnp.maximum(part, 0.0) * (1.0 / CELL)


def kernel(
    rows, cols,
    box_scalar, boxes_hbm, counts_hbm, tails_hbm, doses_hbm, gain_hbm, dose_out, exposure_out,
    boxes, counts, tails, doses, near_x, near_y, edge_x, edge_y, dose_wide,
    gain, gain2, pairs, column, down_t, side_t, across, downward,
    wx2, wy2, wy_own, wy_halo, wx_halo, sens,
    coarse, coarse_t, corner_out, halo_y, halo_x, corner_in,
    in_sem, send_sem, recv_sem,
):
    slots = doses.shape[1]
    tile = gain.shape[0]
    cg = tile // CELL
    r, c = lax.axis_index("row"), lax.axis_index("col")
    halo_y[...] = jnp.zeros_like(halo_y)
    halo_x[...] = jnp.zeros_like(halo_x)
    corner_in[...] = jnp.zeros_like(corner_in)

    def present(dr, dc):
        tests = []
        if dr:
            tests.append(r > 0 if dr < 0 else r < rows - 1)
        if dc:
            tests.append(c > 0 if dc < 0 else c < cols - 1)
        return functools.reduce(jnp.logical_and, tests)

    barrier = pltpu.get_barrier_semaphore()
    for dr, dc in NEAR:
        @pl.when(present(dr, dc))
        def _():
            pl.semaphore_signal(barrier, inc=1, device_id=(r + dr, c + dc), device_id_type=MESH)

    fetches = [
        pltpu.make_async_copy(src, dst, in_sem.at[n])
        for n, (src, dst) in enumerate((
            (boxes_hbm, boxes), (counts_hbm, counts), (tails_hbm, tails), (doses_hbm, doses),
            (gain_hbm, gain),
        ))
    ]
    fetch = fetches[4]
    for one in fetches[:4]:
        one.start()
    fetch.start()
    for one in fetches[:4]:
        one.wait()

    x0, y0, x1, y1 = (boxes[k].astype(jnp.float32) for k in range(4))
    peers = lax.broadcasted_iota(jnp.int32, counts.shape, 1)
    totals = (counts[...] - 1) * BLK + tails[...]
    total = jnp.sum(jnp.where(peers == c, totals, 0), axis=1, keepdims=True)
    live = lax.broadcasted_iota(jnp.int32, (1, slots), 1) < total
    dose = jnp.where(live, doses[...], 0.0)

    stack = jnp.concatenate([x0, x1, y0, y1, dose, dose, dose, dose], axis=0)
    column[...] = jnp.transpose(stack)
    cell_row = lax.broadcasted_iota(jnp.int32, (slots, cg), 1)
    downward[...] = covered(column[:, 2:3], column[:, 3:4], cell_row).astype(jnp.bfloat16)
    side = lax.broadcasted_iota(jnp.int32, (2 * REACH, slots), 0)
    side = jnp.where(side < REACH, side, side + (cg - 2 * REACH))
    side_t[...] = covered(x0, x1, side)
    across[...] = covered(column[:, 0:1], column[:, 1:2], cell_row).astype(jnp.bfloat16)
    down_t[...] = covered(y0, y1, lax.broadcasted_iota(jnp.int32, (cg, slots), 0))
    lane = lax.broadcasted_iota(jnp.int32, (8, LANES), 1)

    def copies(k):
        made = []
        for n, (dr, dc) in enumerate(NEAR):
            ys, xs = (0 if dr < 0 else 1), (0 if dc < 0 else 1)
            if dc == 0:
                src = coarse.at[k, pl.ds(ys * (cg - REACH), REACH), :]
                dst = halo_y.at[k, pl.ds((1 - ys) * REACH, REACH), :]
            elif dr == 0:
                src = coarse_t.at[k, pl.ds(xs * REACH, REACH), :]
                dst = halo_x.at[k, pl.ds((1 - xs) * REACH, REACH), :]
            else:
                src = corner_out.at[k, 2 * xs + ys]
                dst = corner_in.at[k, 2 * (1 - xs) + (1 - ys)]
            made.append(pltpu.make_async_remote_copy(
                src_ref=src, dst_ref=dst,
                send_sem=send_sem.at[k, n], recv_sem=recv_sem.at[k, n],
                device_id=(r + dr, c + dc), device_id_type=MESH,
            ))
        return made

    def send(k, dose, first):
        high, low = halves(side_t[...] * dose)
        both = mxu(jnp.concatenate([high, low], axis=0), downward[...])
        edges = both[:2 * REACH] + both[2 * REACH:]
        coarse_t[k] = edges
        for xs in range(2):
            for ys in range(2):
                packed = jnp.zeros((8, LANES), jnp.float32)
                for q in range(REACH // 8):
                    part = edges[xs * REACH + 8 * q:xs * REACH + 8 * q + 8]
                    shift = (REACH * q - ys * (cg - REACH)) % LANES
                    if shift:
                        part = pltpu.roll(part, shift, 1)
                    packed = jnp.where(lane // REACH == q, part, packed)
                corner_out[k, 2 * xs + ys] = packed
        made = copies(k)
        if first:
            up = (r > 0).astype(jnp.int32) + (r < rows - 1).astype(jnp.int32) + 1
            across_count = (c > 0).astype(jnp.int32) + (c < cols - 1).astype(jnp.int32) + 1
            pl.semaphore_wait(barrier, up * across_count - 1)
        for n in range(2, 8):
            @pl.when(present(*NEAR[n]))
            def _():
                made[n].start()
        high, low = halves(down_t[...] * dose)
        both = mxu(jnp.concatenate([high, low], axis=0), across[...])
        coarse[k] = both[:cg] + both[cg:]
        for n in range(2):
            @pl.when(present(*NEAR[n]))
            def _():
                made[n].start()
        return made

    def weighted(value, weights2, weights):
        high, low = halves(value)
        lhs = jnp.concatenate(
            [jnp.concatenate([high, high], axis=1), jnp.concatenate([low, low], axis=1)], axis=0
        )
        both = mxu(lhs, weights2[...])
        count = value.shape[0]
        return jnp.sum((both[:count] + both[count:]) * weights[...], axis=0, keepdims=True)

    made = send(0, dose, True)

    two_x, two_y = boxes[0] + boxes[2], boxes[1] + boxes[3]
    cell_x, cell_y = two_x >> 3, two_y >> 3
    own = lax.broadcasted_iota(jnp.int32, (cg, slots), 0)
    around = lax.broadcasted_iota(jnp.int32, (2 * REACH, slots), 0)
    around = jnp.where(around < REACH, around - REACH, around + (cg - REACH))
    high, low = halves(spread(own - cell_x))
    wx2[0:cg, :] = high
    wx2[cg:2 * cg, :] = low
    weight = spread(own - cell_y)
    wy_own[...] = weight
    high, low = halves(weight)
    wy2[0:cg, :] = high
    wy2[2 * cg:3 * cg, :] = low
    weight = spread(around - cell_y)
    wy_halo[...] = weight
    high, low = halves(weight)
    blank = jnp.zeros((cg - 2 * REACH, slots), jnp.bfloat16)
    wy2[cg:2 * cg, :] = jnp.concatenate([high, blank], axis=0)
    wy2[3 * cg:4 * cg, :] = jnp.concatenate([low, blank], axis=0)
    wx_halo[...] = spread(around - cell_x)

    blocks = slots // LANES
    group = EDGE_STEP

    def folded(row):
        return jnp.concatenate([row[:, b * LANES:(b + 1) * LANES] for b in range(blocks)], axis=0)

    def flat(square):
        return jnp.concatenate([square[b:b + 1, :] for b in range(blocks)], axis=1)

    for two, near, edges in ((folded(two_x), near_x, edge_x), (folded(two_y), near_y, edge_y)):
        coarse_part = two // (2 * group)
        fine = two - coarse_part * (2 * group)
        for m in range(3):
            for q in range(group):
                gap = fine + ((m - 1) * 2 * group - 2 * q)
                near[m * group + q] = 0.5 * lax.erf(gap.astype(jnp.float32) * (0.5 / FORWARD_RANGE))

        def fill(p, _):
            same, above, below = coarse_part == p, coarse_part == p + 1, coarse_part == p - 1
            far = jnp.where(coarse_part > p, 0.5, -0.5)
            for q in range(group):
                value = jnp.where(above, near[2 * group + q], far)
                value = jnp.where(below, near[q], value)
                edges[p * group + q] = jnp.where(same, near[group + q], value)
            return 0

        lax.fori_loop(0, tile // group + 1, fill, 0)

    def widen(dose):
        for b in range(blocks):
            at = slice(b * LANES, (b + 1) * LANES)
            dose_wide[at, :] = jnp.transpose(jnp.broadcast_to(dose[:, at], (LANES, LANES)))

    zero = tuple(jnp.zeros((blocks, LANES), jnp.float32) for _ in range(4))

    def total_of(sums):
        return flat((sums[0] + sums[1]) + (sums[2] + sums[3]))

    fetch.wait()
    high, low = halves(gain[...])
    gain2[:, 0:tile] = high
    gain2[:, tile:2 * tile] = low
    step = STEP

    def build(g, sums):
        at = pl.ds(pl.multiple_of(g * step, step), step)
        mid_x = (boxes[0, :, at] + boxes[2, :, at]) >> 1
        mid_y = (boxes[1, :, at] + boxes[3, :, at]) >> 1
        pixel = lax.broadcasted_iota(jnp.int32, (tile, step), 0)
        hot = jnp.where(pixel == mid_x, 1.0, 0.0).astype(jnp.bfloat16)
        taken = mxu(gain2[...], jnp.concatenate([hot, hot], axis=0))
        sens[:, at] = jnp.sum(jnp.where(pixel == mid_y, taken, 0.0), axis=0, keepdims=True)
        sums = list(sums)
        for first in range(0, step, UNROLL):
            kept = []
            for n in range(first, first + UNROLL):
                j = g * step + n
                low_x, low_y, high_x, high_y = (box_scalar[k, 0, j] for k in range(4))
                kept.append((edge_x[low_x] - edge_x[high_x]) * (edge_y[low_y] - edge_y[high_y]))
            for n in range(first, first + UNROLL):
                j = g * step + n
                pairs[j] = kept[n - first]
                sums[n % 4] += kept[n - first] * dose_wide[pl.ds(j, 1), :]
        return tuple(sums)

    widen(dose)
    forward = total_of(lax.fori_loop(0, slots // step, build, zero))

    for k in range(ITERS):
        if k:
            made = send(k, dose, False)
            widen(dose)

            def add(g, sums):
                sums = list(sums)
                for n in range(16):
                    j = g * 16 + n
                    sums[n % 4] += pairs[j] * dose_wide[pl.ds(j, 1), :]
                return tuple(sums)

            forward = total_of(lax.fori_loop(0, slots // 16, add, zero))
        background = weighted(coarse[k], wx2, wy_own)
        for n, (dr, dc) in enumerate(NEAR):
            @pl.when(present(-dr, -dc))
            def _():
                made[n].wait_recv()
        background += weighted(halo_y[k], wx2, wy_halo)
        strips = []
        for xs in range(2):
            for q in range(REACH // 8):
                top, low_part = corner_in[k, 2 * xs], corner_in[k, 2 * xs + 1]
                shift = (-REACH * q) % LANES
                if shift:
                    top = pltpu.roll(top, shift, 1)
                shift = (REACH - REACH * q) % LANES
                if shift:
                    low_part = pltpu.roll(low_part, shift, 1)
                strips.append(jnp.where(
                    lane < REACH, top, jnp.where(lane < 2 * REACH, low_part, 0.0)
                ))
        sides = jnp.concatenate([halo_x[k], jnp.concatenate(strips, axis=0)], axis=1)
        background += weighted(sides, wy2, wx_halo)
        exposure = sens[...] * (forward + BACK_RATIO * background) * (1.0 / (1.0 + BACK_RATIO))
        dose = jnp.where(live, dose * TARGET_LEVEL / jnp.where(live, exposure, 1.0), 0.0)
    dose_out[...] = dose
    exposure_out[...] = jnp.where(live, exposure, 0.0)
    for k in range(ITERS):
        made = copies(k)
        for n in range(8):
            @pl.when(present(*NEAR[n]))
            def _():
                made[n].wait_send()


def body(rows, cols, shot_boxes, block_counts, tail_shots, doses, pixel_gain):
    slots = doses.shape[1]
    tile = pixel_gain.shape[0]
    cg = tile // CELL
    f32, bf16 = jnp.float32, jnp.bfloat16
    vmem = pl.BlockSpec(memory_space=pltpu.VMEM)
    return pl.pallas_call(
        functools.partial(kernel, rows, cols),
        out_shape=(jax.ShapeDtypeStruct((1, slots), f32),) * 2,
        in_specs=[pl.BlockSpec(memory_space=pltpu.SMEM)]
        + [pl.BlockSpec(memory_space=pltpu.HBM)] * 5,
        out_specs=(vmem, vmem),
        scratch_shapes=[
            pltpu.VMEM(shot_boxes.shape, jnp.int32),
            pltpu.VMEM(block_counts.shape, jnp.int32),
            pltpu.VMEM(tail_shots.shape, jnp.int32),
            pltpu.VMEM(doses.shape, f32),
            pltpu.VMEM((3 * EDGE_STEP, slots // LANES, LANES), f32),
            pltpu.VMEM((3 * EDGE_STEP, slots // LANES, LANES), f32),
            pltpu.VMEM((tile + EDGE_STEP, slots // LANES, LANES), f32),
            pltpu.VMEM((tile + EDGE_STEP, slots // LANES, LANES), f32),
            pltpu.VMEM((slots, LANES), f32),
            pltpu.VMEM((tile, tile), f32),
            pltpu.VMEM((tile, 2 * tile), bf16),
            pltpu.VMEM((slots, slots // LANES, LANES), f32),
            pltpu.VMEM((slots, 8), f32),
            pltpu.VMEM((cg, slots), f32),
            pltpu.VMEM((2 * REACH, slots), f32),
            pltpu.VMEM((slots, cg), bf16),
            pltpu.VMEM((slots, cg), bf16),
            pltpu.VMEM((2 * cg, slots), bf16),
            pltpu.VMEM((4 * cg, slots), bf16),
            pltpu.VMEM((cg, slots), f32),
            pltpu.VMEM((2 * REACH, slots), f32),
            pltpu.VMEM((2 * REACH, slots), f32),
            pltpu.VMEM((1, slots), f32),
            pltpu.VMEM((ITERS, cg, cg), f32),
            pltpu.VMEM((ITERS, 2 * REACH, cg), f32),
            pltpu.VMEM((ITERS, 4, 8, LANES), f32),
            pltpu.VMEM((ITERS, 2 * REACH, cg), f32),
            pltpu.VMEM((ITERS, 2 * REACH, cg), f32),
            pltpu.VMEM((ITERS, 4, 8, LANES), f32),
            pltpu.SemaphoreType.DMA((5,)),
            pltpu.SemaphoreType.DMA((ITERS, 8)),
            pltpu.SemaphoreType.DMA((ITERS, 8)),
        ],
        compiler_params=pltpu.CompilerParams(
            collective_id=0, has_side_effects=True, vmem_limit_bytes=60 * 1024 * 1024
        ),
    )(shot_boxes, shot_boxes, block_counts, tail_shots, doses, pixel_gain)


def solution(mesh):
    placed = (
        P(None, "row", "col"),
        P("row", None),
        P("row", None),
        P("row", "col"),
        P("row", "col"),
    )
    return jax.shard_map(
        functools.partial(body, mesh.shape["row"], mesh.shape["col"]),
        mesh=mesh,
        in_specs=placed,
        out_specs=(P("row", "col"), P("row", "col")),
        check_vma=False,
    )
```

```python
import functools
import math

import jax
import jax.numpy as jnp
from jax import lax
from jax.experimental import pallas as pl
from jax.experimental.pallas import tpu as pltpu
from jax.sharding import PartitionSpec as P

BLK = 128
ITERS = 3
CELL = 4
BETA = 16
REACH = 32
LANES = 128
EDGE_STEP = 16
UNROLL = 16
STEP = 128

FORWARD_RANGE = 4.0
BACK_RATIO = 0.75
TARGET_LEVEL = 1.0
MESH = pl.DeviceIdType.MESH
NEAR = [(-1, 0), (1, 0), (0, -1), (0, 1), (-1, -1), (-1, 1), (1, -1), (1, 1)]


def halves(value):
    high = value.astype(jnp.bfloat16)
    low = (value - high.astype(jnp.float32)).astype(jnp.bfloat16)
    return high, low


def mxu(a, b):
    return jnp.dot(a, b, preferred_element_type=jnp.float32)


def spread(distance):
    scaled = distance.astype(jnp.float32) / BETA
    inside = jnp.abs(distance) <= REACH
    return jnp.where(inside, jnp.exp(-scaled * scaled) / (math.sqrt(math.pi) * BETA), 0.0)


def covered(low, high, cell):
    edge = cell.astype(jnp.float32) * CELL
    part = jnp.minimum(high, edge + CELL) - jnp.maximum(low, edge)
    return jnp.maximum(part, 0.0) * (1.0 / CELL)


def kernel(
    rows, cols,
    boxes_hbm, counts_hbm, tails_hbm, doses_hbm, gain_hbm, dose_out, exposure_out,
    boxes, counts, tails, doses, box_scalar, near_x, near_y, edge_x, edge_y, dose_wide,
    gain, gain2, pairs, column, down_t, side_t, across, downward,
    wx2, wy2, wy_own, wy_halo, wx_halo, sens,
    coarse, coarse_t, corner_out, halo_y, halo_x, corner_in,
    in_sem, send_sem, recv_sem,
):
    slots = doses.shape[1]
    tile = gain.shape[0]
    cg = tile // CELL
    r, c = lax.axis_index("row"), lax.axis_index("col")
    halo_y[...] = jnp.zeros_like(halo_y)
    halo_x[...] = jnp.zeros_like(halo_x)
    corner_in[...] = jnp.zeros_like(corner_in)

    def present(dr, dc):
        tests = []
        if dr:
            tests.append(r > 0 if dr < 0 else r < rows - 1)
        if dc:
            tests.append(c > 0 if dc < 0 else c < cols - 1)
        return functools.reduce(jnp.logical_and, tests)

    barrier = pltpu.get_barrier_semaphore()
    for dr, dc in NEAR:
        @pl.when(present(dr, dc))
        def _():
            pl.semaphore_signal(barrier, inc=1, device_id=(r + dr, c + dc), device_id_type=MESH)

    fetches = [
        pltpu.make_async_copy(src, dst, in_sem.at[n])
        for n, (src, dst) in enumerate((
            (boxes_hbm, boxes), (counts_hbm, counts), (tails_hbm, tails), (doses_hbm, doses),
            (gain_hbm, gain), (boxes_hbm, box_scalar),
        ))
    ]
    fetch, fetch_scalar = fetches[4:]
    for one in fetches[:4]:
        one.start()
    fetch.start()
    fetch_scalar.start()
    for one in fetches[:4]:
        one.wait()

    x0, y0, x1, y1 = (boxes[k].astype(jnp.float32) for k in range(4))
    peers = lax.broadcasted_iota(jnp.int32, counts.shape, 1)
    totals = (counts[...] - 1) * BLK + tails[...]
    total = jnp.sum(jnp.where(peers == c, totals, 0), axis=1, keepdims=True)
    live = lax.broadcasted_iota(jnp.int32, (1, slots), 1) < total
    dose = jnp.where(live, doses[...], 0.0)

    stack = jnp.concatenate([x0, x1, y0, y1, dose, dose, dose, dose], axis=0)
    column[...] = jnp.transpose(stack)
    cell_row = lax.broadcasted_iota(jnp.int32, (slots, cg), 1)
    downward[...] = covered(column[:, 2:3], column[:, 3:4], cell_row).astype(jnp.bfloat16)
    side = lax.broadcasted_iota(jnp.int32, (2 * REACH, slots), 0)
    side = jnp.where(side < REACH, side, side + (cg - 2 * REACH))
    side_t[...] = covered(x0, x1, side)
    across[...] = covered(column[:, 0:1], column[:, 1:2], cell_row).astype(jnp.bfloat16)
    down_t[...] = covered(y0, y1, lax.broadcasted_iota(jnp.int32, (cg, slots), 0))
    lane = lax.broadcasted_iota(jnp.int32, (8, LANES), 1)

    def copies(k):
        made = []
        for n, (dr, dc) in enumerate(NEAR):
            ys, xs = (0 if dr < 0 else 1), (0 if dc < 0 else 1)
            if dc == 0:
                src = coarse.at[k, pl.ds(ys * (cg - REACH), REACH), :]
                dst = halo_y.at[k, pl.ds((1 - ys) * REACH, REACH), :]
            elif dr == 0:
                src = coarse_t.at[k, pl.ds(xs * REACH, REACH), :]
                dst = halo_x.at[k, pl.ds((1 - xs) * REACH, REACH), :]
            else:
                src = corner_out.at[k, 2 * xs + ys]
                dst = corner_in.at[k, 2 * (1 - xs) + (1 - ys)]
            made.append(pltpu.make_async_remote_copy(
                src_ref=src, dst_ref=dst,
                send_sem=send_sem.at[k, n], recv_sem=recv_sem.at[k, n],
                device_id=(r + dr, c + dc), device_id_type=MESH,
            ))
        return made

    def send(k, dose, first):
        high, low = halves(side_t[...] * dose)
        both = mxu(jnp.concatenate([high, low], axis=0), downward[...])
        edges = both[:2 * REACH] + both[2 * REACH:]
        coarse_t[k] = edges
        for xs in range(2):
            for ys in range(2):
                packed = jnp.zeros((8, LANES), jnp.float32)
                for q in range(REACH // 8):
                    part = edges[xs * REACH + 8 * q:xs * REACH + 8 * q + 8]
                    shift = (REACH * q - ys * (cg - REACH)) % LANES
                    if shift:
                        part = pltpu.roll(part, shift, 1)
                    packed = jnp.where(lane // REACH == q, part, packed)
                corner_out[k, 2 * xs + ys] = packed
        made = copies(k)
        if first:
            up = (r > 0).astype(jnp.int32) + (r < rows - 1).astype(jnp.int32) + 1
            across_count = (c > 0).astype(jnp.int32) + (c < cols - 1).astype(jnp.int32) + 1
            pl.semaphore_wait(barrier, up * across_count - 1)
        for n in range(2, 8):
            @pl.when(present(*NEAR[n]))
            def _():
                made[n].start()
        high, low = halves(down_t[...] * dose)
        both = mxu(jnp.concatenate([high, low], axis=0), across[...])
        coarse[k] = both[:cg] + both[cg:]
        for n in range(2):
            @pl.when(present(*NEAR[n]))
            def _():
                made[n].start()
        return made

    def weighted(value, weights2, weights):
        high, low = halves(value)
        lhs = jnp.concatenate(
            [jnp.concatenate([high, high], axis=1), jnp.concatenate([low, low], axis=1)], axis=0
        )
        both = mxu(lhs, weights2[...])
        count = value.shape[0]
        return jnp.sum((both[:count] + both[count:]) * weights[...], axis=0, keepdims=True)

    made = send(0, dose, True)

    two_x, two_y = boxes[0] + boxes[2], boxes[1] + boxes[3]
    cell_x, cell_y = two_x >> 3, two_y >> 3
    own = lax.broadcasted_iota(jnp.int32, (cg, slots), 0)
    around = lax.broadcasted_iota(jnp.int32, (2 * REACH, slots), 0)
    around = jnp.where(around < REACH, around - REACH, around + (cg - REACH))
    high, low = halves(spread(own - cell_x))
    wx2[0:cg, :] = high
    wx2[cg:2 * cg, :] = low
    weight = spread(own - cell_y)
    wy_own[...] = weight
    high, low = halves(weight)
    wy2[0:cg, :] = high
    wy2[2 * cg:3 * cg, :] = low
    weight = spread(around - cell_y)
    wy_halo[...] = weight
    high, low = halves(weight)
    blank = jnp.zeros((cg - 2 * REACH, slots), jnp.bfloat16)
    wy2[cg:2 * cg, :] = jnp.concatenate([high, blank], axis=0)
    wy2[3 * cg:4 * cg, :] = jnp.concatenate([low, blank], axis=0)
    wx_halo[...] = spread(around - cell_x)

    blocks = slots // LANES
    group = EDGE_STEP

    def folded(row):
        return jnp.concatenate([row[:, b * LANES:(b + 1) * LANES] for b in range(blocks)], axis=0)

    def flat(square):
        return jnp.concatenate([square[b:b + 1, :] for b in range(blocks)], axis=1)

    for two, near, edges in ((folded(two_x), near_x, edge_x), (folded(two_y), near_y, edge_y)):
        coarse_part = two // (2 * group)
        fine = two - coarse_part * (2 * group)
        for m in range(3):
            for q in range(group):
                gap = fine + ((m - 1) * 2 * group - 2 * q)
                near[m * group + q] = 0.5 * lax.erf(gap.astype(jnp.float32) * (0.5 / FORWARD_RANGE))

        def fill(p, _):
            same, above, below = coarse_part == p, coarse_part == p + 1, coarse_part == p - 1
            far = jnp.where(coarse_part > p, 0.5, -0.5)
            for q in range(group):
                value = jnp.where(above, near[2 * group + q], far)
                value = jnp.where(below, near[q], value)
                edges[p * group + q] = jnp.where(same, near[group + q], value)
            return 0

        lax.fori_loop(0, tile // group + 1, fill, 0)

    def widen(dose):
        for b in range(blocks):
            at = slice(b * LANES, (b + 1) * LANES)
            dose_wide[at, :] = jnp.transpose(jnp.broadcast_to(dose[:, at], (LANES, LANES)))

    zero = tuple(jnp.zeros((blocks, LANES), jnp.float32) for _ in range(4))

    def total_of(sums):
        return flat((sums[0] + sums[1]) + (sums[2] + sums[3]))

    fetch.wait()
    fetch_scalar.wait()
    high, low = halves(gain[...])
    gain2[:, 0:tile] = high
    gain2[:, tile:2 * tile] = low
    step = STEP

    def build(g, sums):
        at = pl.ds(pl.multiple_of(g * step, step), step)
        mid_x = (boxes[0, :, at] + boxes[2, :, at]) >> 1
        mid_y = (boxes[1, :, at] + boxes[3, :, at]) >> 1
        pixel = lax.broadcasted_iota(jnp.int32, (tile, step), 0)
        hot = jnp.where(pixel == mid_x, 1.0, 0.0).astype(jnp.bfloat16)
        taken = mxu(gain2[...], jnp.concatenate([hot, hot], axis=0))
        sens[:, at] = jnp.sum(jnp.where(pixel == mid_y, taken, 0.0), axis=0, keepdims=True)
        sums = list(sums)
        for first in range(0, step, UNROLL):
            kept = []
            for n in range(first, first + UNROLL):
                j = g * step + n
                low_x, low_y, high_x, high_y = (box_scalar[k, 0, j] for k in range(4))
                kept.append((edge_x[low_x] - edge_x[high_x]) * (edge_y[low_y] - edge_y[high_y]))
            for n in range(first, first + UNROLL):
                j = g * step + n
                pairs[j] = kept[n - first]
                sums[n % 4] += kept[n - first] * dose_wide[pl.ds(j, 1), :]
        return tuple(sums)

    widen(dose)
    forward = total_of(lax.fori_loop(0, slots // step, build, zero))

    for k in range(ITERS):
        if k:
            made = send(k, dose, False)
            widen(dose)

            def add(g, sums):
                sums = list(sums)
                for n in range(16):
                    j = g * 16 + n
                    sums[n % 4] += pairs[j] * dose_wide[pl.ds(j, 1), :]
                return tuple(sums)

            forward = total_of(lax.fori_loop(0, slots // 16, add, zero))
        background = weighted(coarse[k], wx2, wy_own)
        for n, (dr, dc) in enumerate(NEAR):
            @pl.when(present(-dr, -dc))
            def _():
                made[n].wait_recv()
        background += weighted(halo_y[k], wx2, wy_halo)
        strips = []
        for xs in range(2):
            for q in range(REACH // 8):
                top, low_part = corner_in[k, 2 * xs], corner_in[k, 2 * xs + 1]
                shift = (-REACH * q) % LANES
                if shift:
                    top = pltpu.roll(top, shift, 1)
                shift = (REACH - REACH * q) % LANES
                if shift:
                    low_part = pltpu.roll(low_part, shift, 1)
                strips.append(jnp.where(
                    lane < REACH, top, jnp.where(lane < 2 * REACH, low_part, 0.0)
                ))
        sides = jnp.concatenate([halo_x[k], jnp.concatenate(strips, axis=0)], axis=1)
        background += weighted(sides, wy2, wx_halo)
        exposure = sens[...] * (forward + BACK_RATIO * background) * (1.0 / (1.0 + BACK_RATIO))
        dose = jnp.where(live, dose * TARGET_LEVEL / jnp.where(live, exposure, 1.0), 0.0)
    dose_out[...] = dose
    exposure_out[...] = jnp.where(live, exposure, 0.0)
    for k in range(ITERS):
        made = copies(k)
        for n in range(8):
            @pl.when(present(*NEAR[n]))
            def _():
                made[n].wait_send()


def body(rows, cols, shot_boxes, block_counts, tail_shots, doses, pixel_gain):
    slots = doses.shape[1]
    tile = pixel_gain.shape[0]
    cg = tile // CELL
    f32, bf16 = jnp.float32, jnp.bfloat16
    vmem = pl.BlockSpec(memory_space=pltpu.VMEM)
    return pl.pallas_call(
        functools.partial(kernel, rows, cols),
        out_shape=(jax.ShapeDtypeStruct((1, slots), f32),) * 2,
        in_specs=[pl.BlockSpec(memory_space=pltpu.HBM)] * 5,
        out_specs=(vmem, vmem),
        scratch_shapes=[
            pltpu.VMEM(shot_boxes.shape, jnp.int32),
            pltpu.VMEM(block_counts.shape, jnp.int32),
            pltpu.VMEM(tail_shots.shape, jnp.int32),
            pltpu.VMEM(doses.shape, f32),
            pltpu.SMEM(shot_boxes.shape, jnp.int32),
            pltpu.VMEM((3 * EDGE_STEP, slots // LANES, LANES), f32),
            pltpu.VMEM((3 * EDGE_STEP, slots // LANES, LANES), f32),
            pltpu.VMEM((tile + EDGE_STEP, slots // LANES, LANES), f32),
            pltpu.VMEM((tile + EDGE_STEP, slots // LANES, LANES), f32),
            pltpu.VMEM((slots, LANES), f32),
            pltpu.VMEM((tile, tile), f32),
            pltpu.VMEM((tile, 2 * tile), bf16),
            pltpu.VMEM((slots, slots // LANES, LANES), f32),
            pltpu.VMEM((slots, 8), f32),
            pltpu.VMEM((cg, slots), f32),
            pltpu.VMEM((2 * REACH, slots), f32),
            pltpu.VMEM((slots, cg), bf16),
            pltpu.VMEM((slots, cg), bf16),
            pltpu.VMEM((2 * cg, slots), bf16),
            pltpu.VMEM((4 * cg, slots), bf16),
            pltpu.VMEM((cg, slots), f32),
            pltpu.VMEM((2 * REACH, slots), f32),
            pltpu.VMEM((2 * REACH, slots), f32),
            pltpu.VMEM((1, slots), f32),
            pltpu.VMEM((ITERS, cg, cg), f32),
            pltpu.VMEM((ITERS, 2 * REACH, cg), f32),
            pltpu.VMEM((ITERS, 4, 8, LANES), f32),
            pltpu.VMEM((ITERS, 2 * REACH, cg), f32),
            pltpu.VMEM((ITERS, 2 * REACH, cg), f32),
            pltpu.VMEM((ITERS, 4, 8, LANES), f32),
            pltpu.SemaphoreType.DMA((6,)),
            pltpu.SemaphoreType.DMA((ITERS, 8)),
            pltpu.SemaphoreType.DMA((ITERS, 8)),
        ],
        compiler_params=pltpu.CompilerParams(
            collective_id=0, has_side_effects=True, vmem_limit_bytes=60 * 1024 * 1024
        ),
    )(shot_boxes, block_counts, tail_shots, doses, pixel_gain)


def solution(mesh):
    placed = (
        P(None, "row", "col"),
        P("row", None),
        P("row", None),
        P("row", "col"),
        P("row", "col"),
    )
    return jax.shard_map(
        functools.partial(body, mesh.shape["row"], mesh.shape["col"]),
        mesh=mesh,
        in_specs=placed,
        out_specs=(P("row", "col"), P("row", "col")),
        check_vma=False,
    )
```
